256 devices in a mesh: dp: 32 (over x, z), tensor: 8 (over y, core).
Axes of the slice: x: 4, y: 4, z: 8, core: 2. Of those that a mesh axis runs over, the one named last changes fastest.
Arguments:
- decoder_states: bfloat16 [1024, 16, 4096], P(('dp', 'tensor')), may hold values from -24 to 24
- encoder_memory: bfloat16 [1024, 4, 4096], P('dp', None, 'tensor'), may hold values from -6 to 6
- memory_route: int32 [1024], replicated, may hold values from 0 to 1023, as said below
- memory_length: int32 [1024], replicated, may hold values from 1 to 4
- target_length: int32 [1024], P(('dp', 'tensor')), may hold values from 1 to 16
- objective: int32 [1024], P(('dp', 'tensor')), may hold values from 0 to 2
- mode_table: bfloat16 [3, 4096], replicated, may hold values from -6 to 6
- norm_gain: bfloat16 [4096], replicated, may hold values from 0.5 to 1.5
- w_query: bfloat16 [4096, 2048], P(None, 'tensor'), may hold values from -0.09375 to 0.09375
- w_key: bfloat16 [4096, 2048], P(None, 'tensor'), may hold values from -0.09375 to 0.09375
- w_value: bfloat16 [4096, 2048], P(None, 'tensor'), may hold values from -0.09375 to 0.09375
- w_output: bfloat16 [2048, 4096], P('tensor'), may hold values from -0.125 to 0.125
- cotangent: bfloat16 [1024, 16, 4096], P(('dp', 'tensor')), may hold values from -24 to 24
Outputs:
- layer_output: bfloat16 [1024, 16, 4096], P(('dp', 'tensor'))
- grad_decoder: bfloat16 [1024, 16, 4096], P(('dp', 'tensor'))
- grad_memory: bfloat16 [1024, 4, 4096], P('dp', None, 'tensor')
- grad_query: bfloat16 [4096, 2048], P('dp', 'tensor')
- grad_key: bfloat16 [4096, 2048], P('dp', 'tensor')
- grad_value: bfloat16 [4096, 2048], P('dp', 'tensor')
- grad_output: bfloat16 [2048, 4096], P('tensor', 'dp')
- grad_gain: float32 [4096], replicated
- grad_mode: float32 [3, 4096], replicated
The draws below stay inside these ranges and needn't reach their ends.
Inputs may be any that keep to these rules, and one draw needn't show every extreme that they name: `memory_route`: A permutation of the slots. Slot s belongs to decoder owner s // 32; the examples e with e // 32 equal to one encoder owner send exactly 1 examples to every decoder owner.
All inputs are finite; a program needn't handle non-finite values.
Results may differ from the reference program's by a relative error of at most 0.022.
Values may be sent and summed in bfloat16 or wider, within the bound.
A program may use at most 128 MiB of HBM per device.

```python
import jax
import jax.numpy as jnp
from jax import lax

D = 4096
HD = 256
H = 8
EX_DEV = 32
LD = 16
LE = 4
NEX = 1024
N_DP = 32
N_TENSOR = 8


def draw_memory_route(key, part):
    key = jax.random.fold_in(key, 11)
    owners = NEX // EX_DEV
    per_pair = EX_DEV // owners
    former, latter = jax.random.split(key)
    send_perm = jax.vmap(lambda sub: jax.random.permutation(sub, EX_DEV))(jax.random.split(former, owners))
    recv_perm = jax.vmap(lambda sub: jax.random.permutation(sub, EX_DEV))(jax.random.split(latter, owners))
    target = send_perm // per_pair
    position = send_perm % per_pair
    source = jnp.arange(owners)[:, None]
    place_in = recv_perm[target, source * per_pair + position]
    return (target * EX_DEV + place_in).reshape(NEX).astype(jnp.int32)


def capped_lengths(key, amount, ceiling):
    former, latter = jax.random.split(key)
    lengths = jax.random.randint(former, (amount,), 1, ceiling + 1)
    top_index = jax.random.randint(latter, (), 0, amount)
    return jnp.where(jnp.arange(amount) == top_index, ceiling, lengths).astype(jnp.int32)


def draw_memory_length(key, part):
    key = jax.random.fold_in(key, 23)
    return capped_lengths(key, NEX, LE)


def draw_target_length(key, part):
    key = jax.random.fold_in(key, 37)
    return capped_lengths(key, NEX, LD)


def plant(array, key, smallest, high):
    spot = [jax.random.randint(jax.random.fold_in(key, axis), (), 0, length) for axis, length in enumerate(array.shape)]
    widest = array.shape.index(max(array.shape))
    beside = spot[:widest] + [(spot[widest] + 1) % array.shape[widest]] + spot[widest + 1:]
    return array.at[tuple(spot)].set(smallest).at[tuple(beside)].set(high)


def strengthened(array, rng, source, target, blocks, factor):
    def block_of(axis_at):
        return (jnp.arange(array.shape[axis_at]) // (array.shape[axis_at] // blocks)).reshape((-1,) + (1,) * (array.ndim - 1 - axis_at))

    first = jax.random.permutation(rng, blocks)[block_of(target)]
    other_side = (block_of(target) + blocks // 2) % blocks
    return jnp.where((block_of(source) == first) | (block_of(source) == other_side), factor * array, array)


def block_levels(own_key, dims, cuts, smallest, high):
    loudness, own = 1.0, jax.random.fold_in(own_key, 6)
    for dim, blocks in cuts:
        steps = jnp.exp(jax.random.uniform(jax.random.fold_in(own, dim), (blocks,), jnp.float32, smallest / len(cuts), high / len(cuts)))
        loudness = loudness * jnp.repeat(steps, dims[dim] // blocks).reshape([-1 if axis == dim else 1 for axis in range(len(dims))])
    return loudness


def normal_values(rng, shape, width, limit, cuts=(), dtype=jnp.bfloat16):
    result = jax.random.normal(rng, shape, jnp.float32) * width
    if len(cuts) > 0:
        result = block_levels(rng, shape, cuts, -0.22, 0.18) * result
    return jnp.clip(result, min=-limit, max=limit).astype(dtype)


def gaussian_with(key, dims, spread, most, cuts, heavy, kind=jnp.bfloat16):
    result = spread * jax.random.normal(key, dims, jnp.float32)
    if cuts:
        result = result * block_levels(key, dims, cuts, -0.22, 0.18)
    return jnp.clip(strengthened(result, jax.random.fold_in(key, 3), *heavy), -most, most).astype(kind)


def setup_inputs(seed: int = 0) -> dict:
    key_list = jax.random.split(jax.random.key(seed), 14)
    return {
        "decoder_states": gaussian_with(key_list[0], (NEX, LD, D), 1.0, 24.0, ((0, 256),), (0, 2, 256, 6.0)),
        "encoder_memory": gaussian_with(key_list[1], (NEX, LE, D), 1.0, 6.0, ((0, 32), (2, 8)), (0, 2, 32, 2.75)),
        "memory_route": draw_memory_route(jax.random.fold_in(key_list[13], 71), 0),
        "memory_length": draw_memory_length(jax.random.fold_in(key_list[13], 71), 0),
        "target_length": draw_target_length(jax.random.fold_in(key_list[13], 71), 0),
        "objective": plant(jax.random.randint(key_list[5], (NEX,), 0, 3), jax.random.fold_in(key_list[5], 1), 0, 2).astype(jnp.int32),
        "mode_table": normal_values(key_list[6], (3, D), 1.0, 6.0),
        "norm_gain": jnp.clip(1.0 + 0.1 * jax.random.normal(key_list[7], (D,), jnp.float32), 0.5, 1.5).astype(jnp.bfloat16),
        "w_query": normal_values(key_list[8], (D, H * HD), D ** -0.5, 0.09375, ((1, 8),)),
        "w_key": normal_values(key_list[9], (D, H * HD), D ** -0.5, 0.09375, ((1, 8),)),
        "w_value": normal_values(key_list[10], (D, H * HD), D ** -0.5, 0.09375, ((1, 8),)),
        "w_output": normal_values(key_list[11], (H * HD, D), (H * HD) ** -0.5, 0.125, ((0, 8),)),
        "cotangent": gaussian_with(key_list[12], (NEX, LD, D), 1.0, 24.0, ((0, 256),), (0, 2, 256, 6.0)),
    }


def soft_weights(query_heads, key_heads, valid_keys, score_scale):
    scores = jnp.einsum('bthd,bjhd->bhtj', query_heads.astype(jnp.float32), key_heads.astype(jnp.float32)) * score_scale
    scores = jnp.where(valid_keys[:, None, None, :], scores, -1e+30)
    row_max = lax.optimization_barrier(jnp.max(scores, axis=-1, keepdims=True))
    expo = jnp.exp(scores - row_max)
    return expo / lax.optimization_barrier(jnp.sum(expo, axis=-1, keepdims=True))

def rounded(value):
    return lax.optimization_barrier(value.astype(jnp.bfloat16)).astype(jnp.float32)

def block_sum(left, right, pattern, out_shape):
    left_blocks = left.reshape((N_DP, EX_DEV) + left.shape[1:])
    right_blocks = right.reshape((N_DP, EX_DEV) + right.shape[1:])

    def step(carry, pieces):
        term = jnp.einsum(pattern, pieces[0].astype(jnp.float32), pieces[1].astype(jnp.float32), precision=lax.Precision.HIGHEST)
        return (carry + rounded(term), None)
    total, unused = lax.scan(step, jnp.zeros(out_shape, jnp.float32), (left_blocks, right_blocks))
    return total.astype(jnp.bfloat16)

def reference(decoder_states, encoder_memory, memory_route, memory_length, target_length, objective, mode_table, norm_gain, w_query, w_key, w_value, w_output, cotangent):
    width_dev = H * HD // N_TENSOR
    head_width = H * HD
    score_scale = HD ** (-0.5)
    total = decoder_states.shape[0]
    shifted = decoder_states.astype(jnp.float32) + mode_table.astype(jnp.float32)[objective][:, None, :]
    inv_rms = lax.rsqrt(lax.optimization_barrier(jnp.mean(shifted * shifted, axis=-1, keepdims=True)) + 1e-06)
    normed = shifted * inv_rms
    gain_wide = norm_gain.astype(jnp.float32)
    normed_in = (normed * gain_wide).astype(jnp.bfloat16)
    queries = jnp.dot(normed_in, w_query, preferred_element_type=jnp.float32).astype(jnp.bfloat16)
    placed = jnp.zeros_like(encoder_memory).at[memory_route].set(encoder_memory)
    key_length = jnp.zeros_like(memory_length).at[memory_route].set(memory_length)
    key_rows = jnp.dot(placed, w_key, preferred_element_type=jnp.float32).astype(jnp.bfloat16)
    value_rows = jnp.dot(placed, w_value, preferred_element_type=jnp.float32).astype(jnp.bfloat16)
    query_heads = queries.reshape(total, LD, H, HD)
    key_heads = key_rows.reshape(total, LE, H, HD)
    value_heads = value_rows.reshape(total, LE, H, HD)
    valid_keys = jnp.arange(LE)[None, :] < key_length[:, None]
    probabilities = soft_weights(query_heads, key_heads, valid_keys, score_scale)
    probs_low = probabilities.astype(jnp.bfloat16)
    context_heads = jnp.einsum('bhtj,bjhd->bthd', probs_low.astype(jnp.float32), value_heads.astype(jnp.float32)).astype(jnp.bfloat16)
    context = context_heads.reshape(total, LD, head_width)
    attended = jnp.zeros(shifted.shape, jnp.float32)
    for group in range(N_TENSOR):
        low = group * width_dev
        attended = attended + rounded(jnp.dot(context[:, :, low:low + width_dev], w_output[low:low + width_dev], preferred_element_type=jnp.float32))
    layer_output = (shifted + attended).astype(jnp.bfloat16)
    live_rows = jnp.arange(LD)[None, :] < target_length[:, None]
    masked_cot = jnp.where(live_rows[:, :, None], cotangent, jnp.zeros_like(cotangent))
    grad_context = jnp.einsum('btd,wd->btw', masked_cot.astype(jnp.float32), w_output.astype(jnp.float32)).astype(jnp.bfloat16)
    grad_output = block_sum(context, masked_cot, 'btw,btd->wd', (head_width, D))
    grad_ctx_heads = grad_context.reshape(total, LD, H, HD)
    grad_probs = jnp.einsum('bthd,bjhd->bhtj', grad_ctx_heads.astype(jnp.float32), value_heads.astype(jnp.float32))
    grad_scores = (probabilities * (grad_probs - lax.optimization_barrier(jnp.sum(probabilities * grad_probs, axis=-1, keepdims=True))) * score_scale).astype(jnp.bfloat16)
    grad_q = jnp.einsum('bhtj,bjhd->bthd', grad_scores.astype(jnp.float32), key_heads.astype(jnp.float32)).astype(jnp.bfloat16).reshape(total, LD, head_width)
    grad_k = jnp.einsum('bhtj,bthd->bjhd', grad_scores.astype(jnp.float32), query_heads.astype(jnp.float32)).astype(jnp.bfloat16).reshape(total, LE, head_width)
    grad_v = jnp.einsum('bhtj,bthd->bjhd', probs_low.astype(jnp.float32), grad_ctx_heads.astype(jnp.float32)).astype(jnp.bfloat16).reshape(total, LE, head_width)
    grad_query = block_sum(normed_in, grad_q, 'btd,btw->dw', (D, head_width))
    grad_key = block_sum(placed, grad_k, 'bjd,bjw->dw', (D, head_width))
    grad_value = block_sum(placed, grad_v, 'bjd,bjw->dw', (D, head_width))
    grad_normed = jnp.zeros(shifted.shape, jnp.float32)
    grad_placed = jnp.zeros(placed.shape, jnp.float32)
    for group in range(N_TENSOR):
        low = group * width_dev
        grad_normed = grad_normed + rounded(jnp.einsum('btw,dw->btd', grad_q[:, :, low:low + width_dev].astype(jnp.float32), w_query[:, low:low + width_dev].astype(jnp.float32)))
        memory_term = jnp.einsum('bjw,dw->bjd', grad_k[:, :, low:low + width_dev].astype(jnp.float32), w_key[:, low:low + width_dev].astype(jnp.float32))
        memory_term = memory_term + jnp.einsum('bjw,dw->bjd', grad_v[:, :, low:low + width_dev].astype(jnp.float32), w_value[:, low:low + width_dev].astype(jnp.float32))
        grad_placed = grad_placed + rounded(memory_term)
    grad_memory = grad_placed.astype(jnp.bfloat16)[memory_route]
    scaled = gain_wide * grad_normed
    dot_mean = lax.optimization_barrier(jnp.mean(scaled * normed, axis=-1, keepdims=True))
    grad_shift = masked_cot.astype(jnp.float32) + inv_rms * (scaled - normed * dot_mean)
    grad_decoder = grad_shift.astype(jnp.bfloat16)
    grad_gain = lax.optimization_barrier(jnp.sum(grad_normed * normed, axis=(0, 1)))
    grad_mode = jnp.zeros((3, D), jnp.float32).at[objective].add(lax.optimization_barrier(jnp.sum(grad_shift, axis=1)))
    return (layer_output, grad_decoder, grad_memory, grad_query, grad_key, grad_value, grad_output, grad_gain, grad_mode)
```

```python
import jax
import jax.numpy as jnp
from jax import lax
from jax.experimental import pallas as pl
from jax.experimental.pallas import tpu as pltpu
from jax.sharding import PartitionSpec as P

HD = 256
D = 4096
NX, NZ, NY = 4, 8, 4
NDP, NT = 32, 8
NSEM = 320
BF = jnp.bfloat16
F32 = jnp.float32
MESH = pl.DeviceIdType.MESH
NT_DIMS = (((1,), (1,)), ((), ()))

SCRATCH = {
    "wq": ((D, HD), BF),
    "wk": ((D, HD), BF),
    "wv": ((D, HD), BF),
    "wo": ((HD, D), BF),
    "nall": ((8, 64, D), BF),
    "call": ((8, 64, D), BF),
    "mall": ((8, 128, 512), BF),
    "a_out": ((32, 16, 128), BF),
    "a_in": ((32, 16, 128), BF),
    "b_out": ((32, 16, 128), BF),
    "b_in": ((32, 16, 128), BF),
    "shifted": ((64, D), F32),
    "inv": ((64, 128), F32),
    "q": ((512, HD), BF),
    "k": ((128, HD), BF),
    "v": ((128, HD), BF),
    "ctx": ((8, 64, HD), BF),
    "gctx": ((512, HD), BF),
    "gq": ((8, 64, HD), BF),
    "gk": ((128, HD), BF),
    "gv": ((128, HD), BF),
    "ctx_t": ((HD, 512), BF),
    "gq_t": ((HD, 512), BF),
    "gk_t": ((HD, 128), BF),
    "gv_t": ((HD, 128), BF),
    "p": ((512, 128), F32),
    "sib_out": ((4, 64, D), BF),
    "sib_in": ((4, 64, D), BF),
    "att": ((4, 64, D), BF),
    "att_r": ((2, 64, D), BF),
    "att_l": ((2, 64, D), BF),
    "gn": ((4, 64, D), BF),
    "gn_r": ((2, 64, D), BF),
    "gn_l": ((2, 64, D), BF),
    "msib_out": ((4, 128, 512), BF),
    "msib_in": ((4, 128, 512), BF),
    "mt": ((4, 128, 512), BF),
    "mt_r": ((2, 128, 512), BF),
    "mt_l": ((2, 128, 512), BF),
    "part": ((4, 8, D), F32),
    "s_out": ((8, 8, 256), F32),
    "s_in": ((8, 8, 256), F32),
    "s_x": ((4, 8, 256), F32),
    "s_z": ((8, 8, 256), F32),
    "s_all": ((8, 8, 256), F32),
}
for _name in ("tv", "tq"):
    SCRATCH[_name] = ((8, 1024, 128), BF)
    SCRATCH[_name + "_r"] = ((4, 1024, 128), BF)
    SCRATCH[_name + "_l"] = ((4, 1024, 128), BF)
    SCRATCH[_name + "2"] = ((4, 256, 128), BF)
    SCRATCH[_name + "2_r"] = ((2, 256, 128), BF)
    SCRATCH[_name + "2_l"] = ((2, 256, 128), BF)
for _name in ("to", "tk"):
    SCRATCH[_name] = ((4, 2048, 128), BF)
    SCRATCH[_name + "_r"] = ((2, 2048, 128), BF)
    SCRATCH[_name + "_l"] = ((2, 2048, 128), BF)
    SCRATCH[_name + "2"] = ((8, 256, 128), BF)
    SCRATCH[_name + "2_r"] = ((4, 256, 128), BF)
    SCRATCH[_name + "2_l"] = ((4, 256, 128), BF)


class Links:
    def __init__(self, send, recv):
        self.send, self.recv, self.used, self.started = send, recv, 0, []

    def take(self, count):
        first = self.used
        self.used += count
        assert self.used <= NSEM
        return first

    def at(self, src, dst, index, peer):
        return pltpu.make_async_remote_copy(
            src_ref=src,
            dst_ref=dst,
            send_sem=self.send.at[index],
            recv_sem=self.recv.at[index],
            device_id=peer,
            device_id_type=MESH,
        )

    def copy(self, src, dst, peer):
        return self.at(src, dst, self.take(1), peer)

    def start(self, *copies):
        for one in copies:
            one.start()
            self.started.append(one)

    def finish_sends(self):
        for one in self.started:
            one.wait_send()
        self.started = []


def rows_loop(total, step, body):
    @pl.loop(0, total // step)
    def _(i):
        body(pl.ds(pl.multiple_of(i * step, step), step))


class Gather:
    def __init__(self, links, buf, y, c, right, left, sib):
        half = buf.shape[1] // 2
        h0, h1 = pl.ds(0, half), pl.ds(half, half)
        self.links = links
        mine, lb, rb, fb = ((lax.rem(y + d, NY) * 2 + c) for d in (0, 3, 1, 2))

        def cp(block, rows, peer):
            ref = buf.at[block, rows]
            return links.copy(ref, ref, peer)

        self.r0, self.r1 = cp(mine, h0, right), cp(mine, h1, right)
        self.l0, self.l1 = cp(mine, h0, left), cp(mine, h1, left)
        self.fr, self.fl = cp(lb, h0, right), cp(rb, h1, left)
        self.s_own = links.copy(buf.at[mine], buf.at[mine], sib)
        self.s_l0, self.s_l1 = cp(lb, h0, sib), cp(lb, h1, sib)
        self.s_r0, self.s_r1 = cp(rb, h0, sib), cp(rb, h1, sib)
        self.s_f0, self.s_f1 = cp(fb, h0, sib), cp(fb, h1, sib)

    def own(self):
        self.links.start(self.r0, self.l1, self.r1, self.l0, self.s_own)

    def forward(self):
        self.r0.wait_recv()
        self.links.start(self.fr, self.s_l0)
        self.l1.wait_recv()
        self.links.start(self.fl, self.s_r1)

    def middle(self):
        self.r1.wait_recv()
        self.links.start(self.s_l1)
        self.l0.wait_recv()
        self.links.start(self.s_r0)

    def far(self):
        self.fr.wait_recv()
        self.links.start(self.s_f0)
        self.fl.wait_recv()
        self.links.start(self.s_f1)

    def done(self):
        for one in (self.s_own, self.s_l0, self.s_l1, self.s_r0, self.s_r1, self.s_f0, self.s_f1):
            one.wait_recv()


class Ring:
    def __init__(self, links, buf, from_left, from_right, me, right, left, tile):
        n, rows, _ = buf.shape
        self.links, self.buf, self.me, self.n, self.rows, self.tile = links, buf, me, n, rows, tile
        self.fl, self.fr, self.right, self.left = from_left, from_right, right, left
        self.h = h = n // 2
        half = rows // 2
        self.half = half
        a, b = pl.ds(0, half), pl.ds(half, half)
        far = lax.rem(me + h, n)
        rb, lb = lax.rem(me + h - 1, n), lax.rem(me + n - h + 1, n)
        self.rblk, self.lblk = rb, lb
        self.r1 = links.copy(buf.at[far, a], from_left.at[0, a], right)
        self.l1 = links.copy(buf.at[far, b], from_right.at[0, b], left)
        self.r2i = links.copy(buf.at[rb, b], from_left.at[1, b], right)
        self.l2i = links.copy(buf.at[lb, a], from_right.at[1, a], left)
        self.r2d = links.copy(buf.at[rb, a], from_left.at[1, a], right)
        self.l2d = links.copy(buf.at[lb, b], from_right.at[1, b], left)
        self.rs, self.ls = {}, {}
        for s in range(3, h + 1):
            rr, ll = lax.rem(me + h - s + 1, n), lax.rem(me + n - h + s - 1, n)
            self.rs[s] = links.copy(buf.at[rr], from_left.at[s - 1], right)
            self.ls[s] = links.copy(buf.at[ll], from_right.at[s - 1], left)

    def start_far(self):
        self.links.start(self.r1, self.l1)

    def start_near(self):
        self.links.start(self.r2i, self.l2i)

    def start(self):
        self.start_far()
        self.start_near()

    def add(self, block, arrived, first, count):
        tile = min(self.tile, count)

        @pl.loop(0, count // tile)
        def _(i):
            rows = pl.ds(pl.multiple_of(first + i * tile, tile), tile)
            total = self.buf[block, rows].astype(F32) + arrived[rows].astype(F32)
            self.buf[block, rows] = total.astype(BF)

    def arrive(self, s):
        if s == 2:
            for one in (self.r2i, self.r2d, self.l2i, self.l2d):
                one.wait_recv()
        else:
            self.rs[s].wait_recv()
            self.ls[s].wait_recv()

    def step(self, s):
        n, me, h = self.n, self.me, self.h
        if s == 1:
            self.r1.wait_recv()
            self.add(self.rblk, self.fl.at[0], 0, self.half)
            self.links.start(self.r2d)
            self.l1.wait_recv()
            self.add(self.lblk, self.fr.at[0], self.half, self.half)
            self.links.start(self.l2d)
        else:
            if s == 2:
                self.r2i.wait_recv()
                self.r2d.wait_recv()
            else:
                self.rs[s].wait_recv()
            self.add(lax.rem(me + h - s, n), self.fl.at[s - 1], 0, self.rows)
            self.links.start(self.rs[s + 1])
            if s == 2:
                self.l2i.wait_recv()
                self.l2d.wait_recv()
            else:
                self.ls[s].wait_recv()
            self.add(lax.rem(me + n - h + s, n), self.fr.at[s - 1], 0, self.rows)
            self.links.start(self.ls[s + 1])

    def total(self, rows):
        h = self.h
        return (
            self.buf[self.me, rows].astype(F32)
            + self.fl[h - 1, rows].astype(F32)
            + self.fr[h - 1, rows].astype(F32)
        )


class PairRing:
    def __init__(self, links, out, arrived, buf, from_left, from_right, y, right, left, sib, tile):
        self.links, self.arrived, self.y, self.buf, self.tile = links, arrived, y, buf, tile
        self.order = [lax.rem(y + d, NY) for d in (2, 1, 3, 0)]
        self.copies = [links.copy(out.at[i], arrived.at[i], sib) for i in self.order]
        self.ring = Ring(links, buf, from_left, from_right, y, right, left, tile)

    def send(self):
        self.links.start(*self.copies)

    def pair(self, at):
        self.copies[at].wait_recv()
        block = self.order[at]
        self.ring.add(block, self.arrived.at[block], 0, self.ring.rows)

    def start(self):
        self.pair(0)
        self.ring.start_far()
        self.pair(1)
        self.pair(2)
        self.ring.start_near()
        self.pair(3)


def kernel(*refs):
    (dec, cot, mem, lanes, subs, rowinfo, mode, gain, wq_h, wk_h, wv_h, wo_h) = refs[:12]
    (o_layer, o_dec, o_mem, o_q, o_k, o_v, o_o, o_gm) = refs[12:20]
    S = dict(zip(SCRATCH, refs[20 : 20 + len(SCRATCH)]))
    send_sem, recv_sem, local_sem, credit = refs[20 + len(SCRATCH) :]
    links = Links(send_sem, recv_sem)

    dp, tp = lax.axis_index("dp"), lax.axis_index("tensor")
    x, z = dp // NZ, lax.rem(dp, NZ)
    y, c = tp // 2, lax.rem(tp, 2)
    other = 1 - c
    y_right = (dp, lax.rem(y + 1, NY) * 2 + c)
    y_left = (dp, lax.rem(y + 3, NY) * 2 + c)
    sib = (dp, y * 2 + other)
    x_right = (lax.rem(x + 1, NX) * NZ + z, tp)
    x_left = (lax.rem(x + 3, NX) * NZ + z, tp)
    z_right = (x * NZ + lax.rem(z + 1, NZ), tp)
    z_left = (x * NZ + lax.rem(z + 7, NZ), tp)

    weights = [
        pltpu.make_async_copy(src, S[name], local_sem.at[i])
        for i, (src, name) in enumerate(((wq_h, "wq"), (wk_h, "wk"), (wv_h, "wv"), (wo_h, "wo")))
    ]
    for one in weights:
        one.start()

    barrier = pltpu.get_barrier_semaphore()

    @pl.loop(1, NT)
    def _(i):
        pl.semaphore_signal(barrier, 1, device_id=(dp, lax.rem(tp + i, NT)), device_id_type=MESH)

    @pl.loop(1, NDP)
    def _(i):
        pl.semaphore_signal(barrier, 1, device_id=(lax.rem(dp + i, NDP), tp), device_id_type=MESH)

    nall, call, mall = S["nall"], S["call"], S["mall"]
    gather_n = Gather(links, nall, y, c, y_right, y_left, sib)
    gather_m = Gather(links, mall, y, c, y_right, y_left, sib)
    gather_c = Gather(links, call, y, c, y_right, y_left, sib)
    ring_a = PairRing(links, S["sib_out"], S["sib_in"], S["att"], S["att_r"], S["att_l"], y, y_right, y_left, sib, 16)
    ring_g = PairRing(links, S["sib_out"], S["sib_in"], S["gn"], S["gn_r"], S["gn_l"], y, y_right, y_left, sib, 16)
    ring_m = PairRing(links, S["msib_out"], S["msib_in"], S["mt"], S["mt_r"], S["mt_l"], y, y_right, y_left, sib, 64)

    def weight_rings(name, z_first):
        first = (z, z_right, z_left) if z_first else (x, x_right, x_left)
        second = (x, x_right, x_left) if z_first else (z, z_right, z_left)
        one = Ring(links, S[name], S[name + "_r"], S[name + "_l"], *first, 256)
        two = Ring(links, S[name + "2"], S[name + "2_r"], S[name + "2_l"], *second, 128)
        return one, two

    rings = {name: weight_rings(name, name in ("tv", "tq")) for name in ("tv", "to", "tq", "tk")}

    def prepare(rows):
        kind = rowinfo[rows, 1:2]
        m0, m1, m2 = (mode[i : i + 1, :].astype(F32) for i in range(3))
        shifted = dec[rows, :].astype(F32) + jnp.where(kind == 0, m0, jnp.where(kind == 1, m1, m2))
        S["shifted"][rows, :] = shifted
        inv = lax.rsqrt(jnp.mean(shifted * shifted, axis=1, keepdims=True) + 1e-06)
        S["inv"][rows, :] = jnp.broadcast_to(inv, (16, 128))
        nall[tp, rows] = (shifted * inv * gain[...].astype(F32)).astype(BF)
        at = lax.rem(lax.broadcasted_iota(jnp.int32, (16, 1), 0), 16)
        live = at < rowinfo[rows, 0:1]
        call[tp, rows] = jnp.where(live, cot[rows, :].astype(F32), 0.0).astype(BF)

    rows_loop(64, 16, prepare)

    row = lax.broadcasted_iota(jnp.int32, (512, 128), 0)
    lane = lax.broadcasted_iota(jnp.int32, (512, 128), 1)
    row_t = lax.broadcasted_iota(jnp.int32, (128, 512), 0)
    lane_t = lax.broadcasted_iota(jnp.int32, (128, 512), 1)

    def to_owner(which, f):
        hit = (lanes[which : which + 1, :] == row // 16) & (row % 16 == (lane % 4) * 4 + f)
        return jnp.where(hit, 1.0, 0.0).astype(BF)

    def from_owner(which, f):
        hit = (subs[:, which : which + 1] == lane_t // 16) & (lane_t % 16 == (row_t % 4) * 4 + f)
        return jnp.where(hit, 1.0, 0.0).astype(BF)

    def pack(which, source):
        total = None
        for f in range(4):
            term = jnp.dot(to_owner(which, f), source(f), preferred_element_type=F32)
            total = term if total is None else total + term
        return total.astype(BF).reshape(32, 16, 128)

    S["a_out"][...] = pack(0, lambda f: mem[:, f * 128 : f * 128 + 128])
    S["a_in"][dp] = S["a_out"][dp]

    pl.semaphore_wait(barrier, NT - 1 + NDP - 1)

    def exchange(src, dst, count, me, peer, each):
        first = links.take(count)

        @pl.loop(1, count)
        def _(i):
            to = lax.rem(me + i, count)
            pltpu.make_async_remote_copy(
                src_ref=src.at[each(to)],
                dst_ref=dst.at[me],
                send_sem=send_sem.at[first + to],
                recv_sem=recv_sem.at[first + me],
                device_id=peer(to),
                device_id_type=MESH,
            ).start()

        def wait():
            @pl.loop(1, count)
            def _(i):
                come = lax.rem(me + i, count)
                one = pltpu.make_async_remote_copy(
                    src_ref=src.at[each(come)],
                    dst_ref=dst.at[come],
                    send_sem=send_sem.at[first + come],
                    recv_sem=recv_sem.at[first + come],
                    device_id=peer(come),
                    device_id_type=MESH,
                )
                one.wait_send()
                one.wait_recv()

        return wait

    gather_n.own()
    wait_a = exchange(S["a_out"], S["a_in"], NDP, dp, lambda i: (i, tp), lambda i: i)
    wait_a()
    arrived = S["a_in"][...].reshape(512, 128)
    for f in range(4):
        mall[tp, :, f * 128 : f * 128 + 128] = jnp.dot(
            from_owner(0, f), arrived, preferred_element_type=F32
        ).astype(BF)
    gather_m.own()
    gather_n.forward()
    gather_c.own()
    gather_n.middle()
    gather_m.forward()
    gather_m.middle()
    gather_n.far()
    gather_m.far()
    gather_n.done()

    weights[0].wait()

    @pl.loop(0, 2)
    def _(i):
        rows = nall[pl.ds(i * 4, 4)].reshape(256, D)
        S["q"][pl.ds(pl.multiple_of(i * 256, 256), 256), :] = jnp.dot(
            rows, S["wq"][...], preferred_element_type=F32
        ).astype(BF)

    gather_m.done()
    weights[1].wait()
    weights[2].wait()
    for name, weight in (("k", "wk"), ("v", "wv")):
        total = jnp.zeros((128, HD), F32)
        for t in range(8):
            total += jnp.dot(mall[t], S[weight][t * 512 : t * 512 + 512, :], preferred_element_type=F32)
        S[name][...] = total.astype(BF)

    gather_c.forward()

    scores = lax.dot_general(S["q"][...], S["k"][...], NT_DIMS, preferred_element_type=F32) * (HD**-0.5)
    valid = (row // 16 == lane // 4) & (lane % 4 < lanes[2:3, :])
    scores = jnp.where(valid, scores, -1e30)
    expo = jnp.exp(scores - jnp.max(scores, axis=1, keepdims=True))
    expo = jnp.where(valid, expo, 0.0)
    S["p"][...] = expo / jnp.sum(expo, axis=1, keepdims=True)
    context = jnp.dot(S["p"][...].astype(BF), S["v"][...], preferred_element_type=F32)
    S["ctx"][...] = context.astype(BF).reshape(8, 64, HD)
    S["ctx_t"][...] = context.T.astype(BF)

    gather_c.middle()

    def stacked(name, core):
        return jnp.concatenate([S[name][i * 2 + core] for i in range(NY)], axis=0)

    def wide_terms(name, core, dst, product):
        @pl.loop(0, 8)
        def _(i):
            cols = pl.ds(pl.multiple_of(i * 512, 512), 512)
            dst[:, :, cols] = product(stacked(name, core), cols).astype(BF).reshape(NY, 64, 512)

    def by_output(left, cols):
        return jnp.dot(left, S["wo"][:, cols], preferred_element_type=F32)

    def by_query(left, cols):
        return lax.dot_general(left, S["wq"][cols, :], NT_DIMS, preferred_element_type=F32)

    weights[3].wait()
    wide_terms("ctx", other, S["sib_out"], by_output)
    ring_a.send()
    wide_terms("ctx", c, S["att"], by_output)
    gather_c.far()
    ring_a.start()
    pl.semaphore_signal(credit, 1, device_id=sib, device_id_type=MESH)
    gather_c.done()

    @pl.loop(0, 2)
    def _(i):
        rows = call[pl.ds(i * 4, 4)].reshape(256, D)
        S["gctx"][pl.ds(pl.multiple_of(i * 256, 256), 256), :] = lax.dot_general(
            rows, S["wo"][...], NT_DIMS, preferred_element_type=F32
        ).astype(BF)

    probs = S["p"][...]
    grad_v = jnp.dot(probs.T.astype(BF), S["gctx"][...], preferred_element_type=F32)
    S["gv"][...] = grad_v.astype(BF)
    S["gv_t"][...] = grad_v.T.astype(BF)

    def weight_term(name, left, right):
        z_first = name in ("tv", "tq")

        @pl.loop(0, 8)
        def _(i):
            term = jnp.dot(S[left][...], right(i), preferred_element_type=F32).astype(BF)
            tx, tz = i // 2, lax.rem(i, 2) * 4
            for j in range(4):
                block = term[:, j * 128 : j * 128 + 128]
                if z_first:
                    S[name][tz + j, pl.ds(pl.multiple_of(tx * 256, 256), 256)] = block
                else:
                    S[name][tx, pl.ds(pl.multiple_of((tz + j) * 256, 256), 256)] = block

    def wide(ref):
        return lambda i: ref[:, :, pl.ds(pl.multiple_of(i * 512, 512), 512)].reshape(512, 512)

    weight_term("tv", "gv_t", lambda i: mall[i])
    rings["tv"][0].start()
    weight_term("to", "ctx_t", wide(call))
    rings["to"][0].start()

    probs = S["p"][...]
    grad_p = lax.dot_general(S["gctx"][...], S["v"][...], NT_DIMS, preferred_element_type=F32)
    grad_s = probs * (grad_p - jnp.sum(probs * grad_p, axis=1, keepdims=True)) * (HD**-0.5)
    grad_q = jnp.dot(grad_s.astype(BF), S["k"][...], preferred_element_type=F32)
    S["gq"][...] = grad_q.astype(BF).reshape(8, 64, HD)
    S["gq_t"][...] = grad_q.T.astype(BF)
    grad_k = jnp.dot(grad_s.T.astype(BF), S["q"][...], preferred_element_type=F32)
    S["gk"][...] = grad_k.astype(BF)
    S["gk_t"][...] = grad_k.T.astype(BF)

    weight_term("tq", "gq_t", wide(nall))
    rings["tq"][0].start()
    weight_term("tk", "gk_t", lambda i: mall[i])
    rings["tk"][0].start()

    ring_a.ring.step(1)

    for one in ring_a.copies:
        one.wait_send()
    links.started = [one for one in links.started if all(one is not done for done in ring_a.copies)]
    wide_terms("gq", other, S["sib_out"], by_query)
    pl.semaphore_wait(credit, 1)
    ring_g.send()
    wide_terms("gq", c, S["gn"], by_query)
    rings["tv"][0].step(1)
    ring_g.start()

    def memory_terms(core, dst):
        @pl.loop(0, NY)
        def _(i):
            cols = pl.ds(pl.multiple_of((i * 2 + core) * 512, 512), 512)
            term = lax.dot_general(S["gk"][...], S["wk"][cols, :], NT_DIMS, preferred_element_type=F32)
            term += lax.dot_general(S["gv"][...], S["wv"][cols, :], NT_DIMS, preferred_element_type=F32)
            dst[i] = term.astype(BF)

    memory_terms(other, S["msib_out"])
    ring_m.send()
    memory_terms(c, S["mt"])
    rings["to"][0].step(1)
    rings["tq"][0].step(1)
    rings["tk"][0].step(1)
    ring_m.start()

    rings["tv"][0].step(2)

    ring_a.ring.arrive(2)

    def write_layer(rows):
        o_layer[rows, :] = (S["shifted"][rows, :] + ring_a.ring.total(rows)).astype(BF)

    rows_loop(64, 16, write_layer)

    def second(name):
        one, two = rings[name]
        one.arrive(one.h)
        for i in range(two.n):
            two.buf[i] = one.total(pl.ds(i * 256, 256)).astype(BF)
        two.start()

    ring_g.ring.step(1)
    second("to")
    rings["tq"][0].step(2)
    ring_m.ring.step(1)
    rings["tv"][0].step(3)
    second("tk")
    rings["tq"][0].step(3)
    rings["to"][1].step(1)
    rings["tk"][1].step(1)

    S["part"][...] = jnp.zeros_like(S["part"])
    ring_g.ring.arrive(2)

    def write_dec(rows):
        grad = ring_g.ring.total(rows)
        inv = S["inv"][rows, 0:1]
        normed = S["shifted"][rows, :] * inv
        product = grad * normed
        wide_gain = gain[...].astype(F32)
        dot_mean = jnp.mean(wide_gain * product, axis=1, keepdims=True)
        shift = call[tp, rows].astype(F32) + inv * (wide_gain * grad - normed * dot_mean)
        o_dec[rows, :] = shift.astype(BF)
        kind = rowinfo[rows, 1:2]
        S["part"][0] += product[0:8] + product[8:16]
        for i in range(3):
            own = jnp.where(kind == i, shift, 0.0)
            S["part"][i + 1] += own[0:8] + own[8:16]

    rows_loop(64, 16, write_dec)
    for i in range(4):
        total = jnp.sum(S["part"][i], axis=0, keepdims=True)
        for t in range(8):
            S["s_out"][t, i : i + 1, :] = total[:, t * 512 : t * 512 + 256]
            S["s_out"][t, i + 4 : i + 5, :] = total[:, t * 512 + 256 : t * 512 + 512]
    S["s_in"][tp] = S["s_out"][tp]
    wait_s = exchange(S["s_out"], S["s_in"], NT, tp, lambda i: (dp, i), lambda i: i)

    ring_m.ring.arrive(2)
    back = ring_m.ring.total(pl.ds(0, 128)).astype(BF)
    S["b_out"][...] = pack(1, lambda f: back[:, f * 128 : f * 128 + 128])
    S["b_in"][dp] = S["b_out"][dp]
    wait_b = exchange(S["b_out"], S["b_in"], NDP, dp, lambda i: (i, tp), lambda i: i)

    second("tv")
    wait_s()
    S["s_x"][x] = jnp.sum(S["s_in"][...], axis=0)
    wait_x = exchange(S["s_x"], S["s_x"], NX, x, lambda i: (i * NZ + z, tp), lambda i: x)
    second("tq")
    rings["to"][1].step(2)
    rings["tk"][1].step(2)
    wait_x()
    S["s_z"][z] = jnp.sum(S["s_x"][...], axis=0)
    wait_z = exchange(S["s_z"], S["s_z"], NZ, z, lambda i: (x * NZ + i, tp), lambda i: z)
    rings["tv"][1].step(1)
    rings["tq"][1].step(1)
    rings["to"][1].step(3)
    rings["tk"][1].step(3)
    wait_z()
    S["s_all"][tp] = jnp.sum(S["s_z"][...], axis=0)
    wait_t = exchange(S["s_all"], S["s_all"], NT, tp, lambda i: (dp, i), lambda i: tp)

    wait_b()
    arrived = S["b_in"][...].reshape(512, 128)
    for f in range(4):
        o_mem[:, f * 128 : f * 128 + 128] = jnp.dot(
            from_owner(1, f), arrived, preferred_element_type=F32
        ).astype(BF)

    for name, dst in (("tv", o_v), ("tq", o_q), ("to", o_o), ("tk", o_k)):
        ring = rings[name][1]
        ring.arrive(ring.h)
        total = ring.total(pl.ds(0, 256))
        dst[...] = (total if name == "to" else total.T).astype(BF)

    wait_t()
    for t in range(8):
        o_gm[:, t * 512 : t * 512 + 256] = S["s_all"][t, 0:4, :]
        o_gm[:, t * 512 + 256 : t * 512 + 512] = S["s_all"][t, 4:8, :]
    links.finish_sends()


def shards(
    decoder_states,
    encoder_memory,
    memory_route,
    memory_length,
    target_length,
    objective,
    mode_table,
    norm_gain,
    w_query,
    w_key,
    w_value,
    w_output,
    cotangent,
):
    me = lax.axis_index("dp")
    own_owner = lax.dynamic_slice_in_dim(memory_route, me * 32, 32, 0) // 32
    hit = memory_route[None, :] == (me * 32 + jnp.arange(32, dtype=jnp.int32))[:, None]
    source = jnp.sum(jnp.where(hit, jnp.arange(1024, dtype=jnp.int32)[None, :] // 32, 0), axis=1)
    length = jnp.sum(jnp.where(hit, memory_length[None, :], 0), axis=1)
    lanes = jnp.repeat(jnp.stack([own_owner, source, length]), 4, axis=1)
    subs = jnp.repeat(jnp.stack([source, own_owner], axis=1), 4, axis=0)
    rowinfo = jnp.repeat(jnp.stack([target_length, objective], axis=1), 16, axis=0)

    vmem = pl.BlockSpec(memory_space=pltpu.VMEM)
    hbm = pl.BlockSpec(memory_space=pl.ANY)
    shape = jax.ShapeDtypeStruct
    layer, dec, mem, gq, gk, gv, go, gm = pl.pallas_call(
        kernel,
        out_shape=[
            shape((64, D), BF),
            shape((64, D), BF),
            shape((128, 512), BF),
            shape((128, HD), BF),
            shape((128, HD), BF),
            shape((128, HD), BF),
            shape((HD, 128), BF),
            shape((4, D), F32),
        ],
        in_specs=[vmem] * 8 + [hbm] * 4,
        out_specs=[vmem] * 8,
        scratch_shapes=[pltpu.VMEM(*spec) for spec in SCRATCH.values()]
        + [
            pltpu.SemaphoreType.DMA((NSEM,)),
            pltpu.SemaphoreType.DMA((NSEM,)),
            pltpu.SemaphoreType.DMA((4,)),
            pltpu.SemaphoreType.REGULAR,
        ],
        compiler_params=pltpu.CompilerParams(
            collective_id=0, has_side_effects=True, vmem_limit_bytes=62 * 1024 * 1024
        ),
        cost_estimate=pl.CostEstimate(flops=8 * 10**9, bytes_accessed=12 * 10**6, transcendentals=10**5),
    )(
        decoder_states.reshape(64, D),
        cotangent.reshape(64, D),
        encoder_memory.reshape(128, 512),
        lanes,
        subs,
        rowinfo,
        mode_table,
        norm_gain.reshape(1, D),
        w_query,
        w_key,
        w_value,
        w_output,
    )
    return (
        layer.reshape(4, 16, D),
        dec.reshape(4, 16, D),
        mem.reshape(32, 4, 512),
        gq,
        gk,
        gv,
        go,
        gm[0],
        gm[1:4],
    )


def solution(mesh):
    return jax.shard_map(
        shards,
        mesh=mesh,
        in_specs=(
            P(("dp", "tensor"), None, None),
            P("dp", None, "tensor"),
            P(),
            P(),
            P(("dp", "tensor")),
            P(("dp", "tensor")),
            P(),
            P(),
            P(None, "tensor"),
            P(None, "tensor"),
            P(None, "tensor"),
            P("tensor", None),
            P(("dp", "tensor"), None, None),
        ),
        out_specs=(
            P(("dp", "tensor"), None, None),
            P(("dp", "tensor"), None, None),
            P("dp", None, "tensor"),
            P("dp", "tensor"),
            P("dp", "tensor"),
            P("dp", "tensor"),
            P("tensor", "dp"),
            P(),
            P(),
        ),
        check_vma=False,
    )
```

```python
import types

import jax
import jax.numpy as jnp
from jax import lax
from jax.experimental import pallas as pl
from jax.experimental.pallas import tpu as pltpu
from jax.sharding import PartitionSpec as P

HD = 256
D = 4096
NX, NZ, NY = 4, 8, 4
NDP, NT = 32, 8
BF = jnp.bfloat16
F32 = jnp.float32
MESH = pl.DeviceIdType.MESH
NT_DIMS = (((1,), (1,)), ((), ()))

SOURCES = dict(
    i_mode=((3, D), BF),
    i_gain=((32, 128), BF),
    i_dec=((4, 16, D), BF),
    i_route=((8, 128), jnp.int32),
    i_lengths=((8, 128), jnp.int32),
    i_mem=((32, 4, 512), BF),
    i_cot=((4, 16, D), BF),
    wq=((D, HD), BF),
    wk=((D, HD), BF),
    wv=((D, HD), BF),
    wo=((HD, D), BF),
)
RESULTS = dict(
    r_layer=((4, 16, D), BF),
    r_dec=((4, 16, D), BF),
    r_mem=((32, 4, 512), BF),
    r_q=((128, HD), BF),
    r_k=((128, HD), BF),
    r_v=((128, HD), BF),
    r_o=((HD, 128), BF),
    r_gain=((32, 128), F32),
    r_mode=((3, D), F32),
)
BUFFERS = dict(
    nall=((8, 64, D), BF),
    call=((2, 8, 64, D // 2), BF),
    mall=((8, 128, 512), BF),
    a_out=((32, 16, 128), BF),
    a_in=((32, 16, 128), BF),
    b_out=((32, 16, 128), BF),
    b_in=((32, 16, 128), BF),
    shifted=((64, D), F32),
    inv=((64, 128), F32),
    q=((512, HD), BF),
    k=((128, HD), BF),
    v=((128, HD), BF),
    ctx=((8, 64, HD), BF),
    gctx=((512, HD), BF),
    gq=((8, 64, HD), BF),
    gk=((128, HD), BF),
    gv=((128, HD), BF),
    ctx_t=((HD, 512), BF),
    gq_t=((HD, 512), BF),
    gk_t=((HD, 128), BF),
    gv_t=((HD, 128), BF),
    p=((512, 128), F32),
    sib_out=((4, 64, D), BF),
    sib_in=((4, 64, D), BF),
    att=((4, 64, D), BF),
    att_r=((2, 64, D), BF),
    att_l=((2, 64, D), BF),
    gn=((4, 64, D), BF),
    gn_r=((2, 64, D), BF),
    gn_l=((2, 64, D), BF),
    msib_out=((4, 128, 512), BF),
    msib_in=((4, 128, 512), BF),
    mt=((4, 128, 512), BF),
    mt_r=((2, 128, 512), BF),
    mt_l=((2, 128, 512), BF),
    part=((4, 8, D), F32),
    s_out=((8, 8, 256), F32),
    s_in=((8, 8, 256), F32),
    s_x=((4, 8, 256), F32),
    s_z=((8, 8, 256), F32),
    s_all=((8, 8, 256), F32),
    gain=((1, D), F32),
    lanes=((128, 128), F32),
    cols=((128, 128), F32),
    back=((32, 4, 512), F32),
)
SCRATCH = SOURCES | RESULTS | BUFFERS
X_ROWS = (160, 160, 160, 128)

NSEND, NRECV = 32, 85


def ring_buffers(n, rows):
    return [((n, rows, 128), BF), ((n // 2, rows, 128), BF), ((n // 2, rows, 128), BF)]


def term_buffers(xr):
    zr = HD - xr
    found = ring_buffers(NX, NZ * xr) + ring_buffers(NZ, xr)
    return found + (ring_buffers(NZ, NX * zr) + ring_buffers(NX, zr) if zr else [])


TERM_BUFFERS = [term_buffers(xr) for xr in X_ROWS]
FLAT = list(SCRATCH.values()) + [one for term in TERM_BUFFERS for one in term]


class Links:
    def __init__(self, send, recv):
        self.send, self.recv, self.sends, self.recvs, self.open = send, recv, 0, 0, []

    def new_send(self):
        self.sends += 1
        assert self.sends <= NSEND
        return self.sends - 1

    def new_recv(self):
        self.recvs += 1
        assert self.recvs <= NRECV
        return self.recvs - 1

    def copy(self, src, dst, send, recv, peer):
        return pltpu.make_async_remote_copy(
            src_ref=src,
            dst_ref=dst,
            send_sem=self.send.at[send],
            recv_sem=self.recv.at[recv],
            device_id=peer,
            device_id_type=MESH,
        )

    def arrived(self, recv, ref, peer):
        self.copy(ref, ref, 0, recv, peer).wait_recv()

    def sent(self, send, ref, peer):
        self.copy(ref, ref, send, 0, peer).wait_send()

    def finish_sends(self):
        for one in self.open:
            self.sent(*one)
        self.open = []


class Gather:
    def __init__(self, links, buf, y, c, right, left, sib):
        half = buf.shape[1] // 2
        self.h0, self.h1 = pl.ds(0, half), pl.ds(half, half)
        self.links, self.buf, self.complete = links, buf, False
        self.right, self.left, self.sib = right, left, sib
        self.mine, self.lb, self.rb, self.fb = (lax.rem(y + d, NY) * 2 + c for d in (0, 3, 1, 2))
        self.send = links.new_send()
        self.near, self.mid, self.last, self.pair = (links.new_recv() for _ in range(4))

    def push(self, block, rows, recv, peer):
        ref = self.buf.at[block, rows]
        self.links.copy(ref, ref, self.send, recv, peer).start()

    def wait(self, recv, blocks):
        self.links.arrived(recv, self.buf.at[pl.ds(0, blocks)], self.sib)

    def own(self):
        self.push(self.mine, self.h0, self.near, self.right)
        self.push(self.mine, self.h1, self.near, self.left)
        self.push(self.mine, self.h1, self.mid, self.right)
        self.push(self.mine, self.h0, self.mid, self.left)
        ref = self.buf.at[self.mine]
        self.links.copy(ref, ref, self.send, self.pair, self.sib).start()
        self.links.open.append((self.send, self.buf.at[pl.ds(0, 7)], self.sib))

    def forward(self):
        self.wait(self.near, 1)
        self.push(self.lb, self.h0, self.last, self.right)
        self.push(self.rb, self.h1, self.last, self.left)
        self.push(self.lb, self.h0, self.pair, self.sib)
        self.push(self.rb, self.h1, self.pair, self.sib)

    def middle(self):
        self.wait(self.mid, 1)
        self.push(self.lb, self.h1, self.pair, self.sib)
        self.push(self.rb, self.h0, self.pair, self.sib)

    def far(self):
        self.wait(self.last, 1)
        self.push(self.fb, self.h0, self.pair, self.sib)
        self.push(self.fb, self.h1, self.pair, self.sib)

    def done(self):
        if not self.complete:
            self.complete = True
            self.wait(self.pair, 4)


class Ring:
    def __init__(self, links, buf, from_left, from_right, me, right, left, tile):
        self.n, self.rows, _ = buf.shape
        self.links, self.buf, self.me, self.tile = links, buf, me, tile
        self.fl, self.fr, self.right, self.left = from_left, from_right, right, left
        self.h = self.n // 2
        self.half = self.rows // 2
        self.a, self.b = pl.ds(0, self.half), pl.ds(self.half, self.half)
        self.send = links.new_send()
        self.stage = [None] + [links.new_recv() for _ in range(self.h)]

    def at(self, distance):
        return lax.rem(self.me + distance + self.n, self.n)

    def push_right(self, stage, rows):
        src = self.buf.at[self.at(self.h + 1 - stage), rows]
        self.links.copy(src, self.fl.at[stage - 1, rows], self.send, self.stage[stage], self.right).start()

    def push_left(self, stage, rows):
        src = self.buf.at[self.at(stage - 1 - self.h), rows]
        self.links.copy(src, self.fr.at[stage - 1, rows], self.send, self.stage[stage], self.left).start()

    def start_far(self):
        self.push_right(1, self.a)
        self.push_left(1, self.b)
        self.links.open.append((self.send, self.buf.at[pl.ds(0, self.n - 1)], self.right))

    def start_near(self):
        self.push_right(2, self.b)
        self.push_left(2, self.a)

    def start(self):
        self.start_far()
        self.start_near()

    def add(self, block, arrived, first, count):
        tile = min(self.tile, count)

        @pl.loop(0, count // tile)
        def _(i):
            rows = pl.ds(pl.multiple_of(first + i * tile, tile), tile)
            total = self.buf[block, rows].astype(F32) + arrived[rows].astype(F32)
            self.buf[block, rows] = total.astype(BF)

    def arrive(self, stage):
        blocks = 1 if stage == 1 else 2
        self.links.arrived(self.stage[stage], self.buf.at[pl.ds(0, blocks)], self.right)

    def step(self, stage):
        self.arrive(stage)
        whole = pl.ds(0, self.rows)
        if stage == 1:
            self.add(self.at(self.h - 1), self.fl.at[0], 0, self.half)
            self.push_right(2, self.a)
            self.add(self.at(1 - self.h), self.fr.at[0], self.half, self.half)
            self.push_left(2, self.b)
        else:
            self.add(self.at(self.h - stage), self.fl.at[stage - 1], 0, self.rows)
            self.push_right(stage + 1, whole)
            self.add(self.at(stage - self.h), self.fr.at[stage - 1], 0, self.rows)
            self.push_left(stage + 1, whole)

    def total(self, rows):
        h = self.h
        return (
            self.buf[self.me, rows].astype(F32)
            + self.fl[h - 1, rows].astype(F32)
            + self.fr[h - 1, rows].astype(F32)
        )


class PairRing:
    def __init__(self, links, out, arrived, buf, from_left, from_right, y, right, left, sib, tile):
        self.links, self.out, self.arrived, self.sib = links, out, arrived, sib
        self.order = [lax.rem(y + d, NY) for d in (2, 1, 3, 0)]
        self.sending = links.new_send()
        self.coming = [links.new_recv() for _ in range(3)]
        self.ring = Ring(links, buf, from_left, from_right, y, right, left, tile)

    def send(self):
        for i, recv in zip(self.order, (0, 1, 1, 2)):
            self.links.copy(self.out.at[i], self.arrived.at[i], self.sending, self.coming[recv], self.sib).start()
        self.links.open.append((self.sending, self.out, self.sib))

    def sent(self):
        self.links.sent(self.sending, self.out, self.sib)
        self.links.open = [one for one in self.links.open if one[0] != self.sending]

    def pair(self, recv, blocks):
        self.links.arrived(self.coming[recv], self.arrived.at[pl.ds(0, len(blocks))], self.sib)
        for block in blocks:
            self.ring.add(block, self.arrived.at[block], 0, self.ring.rows)

    def start(self):
        self.pair(0, self.order[:1])
        self.ring.start_far()
        self.pair(1, self.order[1:3])
        self.ring.start_near()
        self.pair(2, self.order[3:])


class Term:
    def __init__(self, links, xr, refs, x, z, on_x, on_z, left, right, out, flip):
        self.x, self.xr, self.zr, self.left, self.right, self.out, self.flip = x, xr, HD - xr, left, right, out, flip
        zr = self.zr
        self.xf = Ring(links, *refs[0:3], *on_x, 2 * xr)
        self.xs = Ring(links, *refs[3:6], *on_z, xr // 2)
        self.zf = self.zs = None
        if zr:
            self.zf = Ring(links, *refs[6:9], *on_z, 2 * zr)
            self.zs = Ring(links, *refs[9:12], *on_x, zr // 2)

    def tile(self, tx, half):
        term = jnp.dot(self.left[...], self.right(tx, half), preferred_element_type=F32).astype(BF)
        for j in range(4):
            tz = half * 4 + j
            block = term[:, j * 128 : j * 128 + 128]
            self.xf.buf[tx, pl.ds(pl.multiple_of(tz * self.xr, self.xr), self.xr)] = block[0 : self.xr]
            if self.zr:
                self.zf.buf[tz, pl.ds(pl.multiple_of(tx * self.zr, self.zr), self.zr)] = block[self.xr :]

    def first(self):
        @pl.loop(0, 2)
        def _(i):
            self.tile(lax.rem(self.x + 2, NX), i)

        self.xf.start_far()

    def near(self):
        @pl.loop(0, 4)
        def _(i):
            self.tile(lax.rem(self.x + 1 + (i // 2) * 2, NX), lax.rem(i, 2))

        self.xf.start_near()

    def own(self):
        @pl.loop(0, 2)
        def _(i):
            self.tile(self.x, i)

        if self.zr:
            self.zf.start()

    def second(self, one, two, rows):
        one.arrive(one.h)
        for i in range(two.n):
            two.buf[i] = one.total(pl.ds(i * rows, rows)).astype(BF)
        two.start()

    def to_z(self):
        self.second(self.xf, self.xs, self.xr)

    def to_x(self):
        self.second(self.zf, self.zs, self.zr)

    def result(self, copy):
        parts = [(self.xs, self.xr)] + ([(self.zs, self.zr)] if self.zr else [])
        for ring, _ in parts:
            ring.arrive(ring.h)
        total = jnp.concatenate([ring.total(pl.ds(0, rows)) for ring, rows in parts], axis=0)
        self.out[...] = (total.T if self.flip else total).astype(BF)
        copy.start()


def kernel(*refs):
    target, objective = refs[:2]
    count = len(SOURCES), len(RESULTS), len(SCRATCH), len(FLAT)
    sources, outs = refs[2 : 2 + count[0]], refs[2 + count[0] : 2 + count[0] + count[1]]
    held = refs[2 + count[0] + count[1] :]
    S = types.SimpleNamespace(**dict(zip(SCRATCH, held)))
    of_terms = iter(held[count[2] : count[3]])
    send_sem, recv_sem, local_sem, credit = held[count[3] :]
    links = Links(send_sem, recv_sem)

    dp, tp = lax.axis_index("dp"), lax.axis_index("tensor")
    x, z = dp // NZ, lax.rem(dp, NZ)
    y, c = tp // 2, lax.rem(tp, 2)
    other = 1 - c
    y_right = (dp, lax.rem(y + 1, NY) * 2 + c)
    y_left = (dp, lax.rem(y + 3, NY) * 2 + c)
    sib = (dp, y * 2 + other)
    x_right = (lax.rem(x + 1, NX) * NZ + z, tp)
    x_left = (lax.rem(x + 3, NX) * NZ + z, tp)
    z_right = (x * NZ + lax.rem(z + 1, NZ), tp)
    z_left = (x * NZ + lax.rem(z + 7, NZ), tp)

    arriving, results = types.SimpleNamespace(), types.SimpleNamespace()
    for i, name in enumerate(SOURCES):
        setattr(arriving, name, pltpu.make_async_copy(sources[i], held[i], local_sem.at[i]))
    for i, name in enumerate(RESULTS):
        copy = pltpu.make_async_copy(held[count[0] + i], outs[i], local_sem.at[count[0] + i])
        setattr(results, name, copy)
    loaded = list(vars(arriving).values())
    for one in loaded[:3]:
        one.start()

    def need(*copies):
        for one in copies:
            if any(one is other for other in loaded):
                loaded[:] = [other for other in loaded if other is not one]
                one.wait()

    barrier = pltpu.get_barrier_semaphore()

    @pl.loop(1, NT)
    def _(i):
        pl.semaphore_signal(barrier, 1, device_id=(dp, lax.rem(tp + i, NT)), device_id_type=MESH)

    @pl.loop(1, NDP)
    def _(i):
        pl.semaphore_signal(barrier, 1, device_id=(lax.rem(dp + i, NDP), tp), device_id_type=MESH)

    for one in loaded[3:]:
        one.start()

    nall, call, mall = S.nall, S.call, S.mall
    gather_n = Gather(links, nall, y, c, y_right, y_left, sib)
    gather_m = Gather(links, mall, y, c, y_right, y_left, sib)
    early = 1 - x // 2
    gather_0 = Gather(links, call.at[early], y, c, y_right, y_left, sib)
    gather_1 = Gather(links, call.at[1 - early], y, c, y_right, y_left, sib)
    ring_a = PairRing(links, S.sib_out, S.sib_in, S.att, S.att_r, S.att_l, y, y_right, y_left, sib, 16)
    ring_g = PairRing(links, S.sib_out, S.sib_in, S.gn, S.gn_r, S.gn_l, y, y_right, y_left, sib, 16)
    ring_m = PairRing(links, S.msib_out, S.msib_in, S.mt, S.mt_r, S.mt_l, y, y_right, y_left, sib, 64)

    def by_context(tx, half):
        cols = pl.ds(pl.multiple_of(lax.rem(tx, 2) * 1024 + half * 512, 512), 512)
        return call[tx // 2, :, :, cols].reshape(512, 512)

    def by_normed(tx, half):
        return nall[:, :, pl.ds(pl.multiple_of(tx * 1024 + half * 512, 512), 512)].reshape(512, 512)

    def by_memory(tx, half):
        return mall[tx * 2 + half]

    on_x, on_z = (x, x_right, x_left), (z, z_right, z_left)
    to, tv, tq, tk = (
        Term(links, xr, [next(of_terms) for _ in spec], x, z, on_x, on_z, left, right, out, flip)
        for xr, spec, left, right, out, flip in zip(
            X_ROWS,
            TERM_BUFFERS,
            (S.ctx_t, S.gv_t, S.gq_t, S.gk_t),
            (by_context, by_memory, by_normed, by_memory),
            (S.r_o, S.r_v, S.r_q, S.r_k),
            (False, True, True, True),
        )
    )

    need(arriving.i_mode, arriving.i_gain, arriving.i_dec)
    wide_gain = jnp.concatenate([S.i_gain[i : i + 1, :].astype(F32) for i in range(32)], axis=1)
    S.gain[...] = wide_gain

    @pl.loop(0, 4)
    def _(i):
        rows = pl.ds(pl.multiple_of(i * 16, 16), 16)
        kind = jnp.full((1, D), objective[i], jnp.int32)
        m0, m1, m2 = (S.i_mode[j : j + 1, :].astype(F32) for j in range(3))
        shifted = S.i_dec[i].astype(F32) + jnp.where(kind == 0, m0, jnp.where(kind == 1, m1, m2))
        S.shifted[rows, :] = shifted
        inv = lax.rsqrt(jnp.mean(shifted * shifted, axis=1, keepdims=True) + 1e-06)
        S.inv[rows, :] = jnp.broadcast_to(inv, (16, 128))
        nall[tp, rows] = (shifted * inv * S.gain[...]).astype(BF)

    pl.semaphore_wait(barrier, NT - 1 + NDP - 1)

    row = lax.broadcasted_iota(jnp.int32, (512, 128), 0)
    lane = lax.broadcasted_iota(jnp.int32, (512, 128), 1)
    row_t = lax.broadcasted_iota(jnp.int32, (128, 512), 0)
    lane_t = lax.broadcasted_iota(jnp.int32, (128, 512), 1)

    def pack(which, rows):
        total = None
        match = S.lanes[which : which + 1, :].astype(jnp.int32) == row // 16
        for f in range(4):
            hot = jnp.where(match & (row % 16 == (lane // 32) * 4 + f), 1.0, 0.0).astype(BF)
            term = jnp.dot(hot, rows[:, f * 128 : f * 128 + 128], preferred_element_type=F32)
            total = term if total is None else total + term
        return total.astype(BF).reshape(32, 16, 128)

    def unpack(which, packed):
        match = S.cols[:, which : which + 1].astype(jnp.int32) == lane_t // 16
        parts = []
        for f in range(4):
            hot = jnp.where(match & (lane_t % 16 == (row_t // 32) * 4 + f), 1.0, 0.0).astype(BF)
            parts.append(jnp.dot(hot, packed, preferred_element_type=F32))
        return jnp.concatenate(parts, axis=1)

    def exchange(src, dst, count, me, peer, each):
        send, recv = links.new_send(), links.new_recv()

        @pl.loop(1, count)
        def _(i):
            to = lax.rem(me + i, count)
            links.copy(src.at[each(to)], dst.at[me], send, recv, peer(to)).start()

        def wait():
            others = dst.at[pl.ds(0, count - 1)]
            links.sent(send, others, sib)
            links.arrived(recv, others, sib)

        return wait

    waits = types.SimpleNamespace()

    def send_examples():
        need(arriving.i_route, arriving.i_lengths, arriving.i_mem)
        at = lax.broadcasted_iota(jnp.int32, (32, 128), 1)
        entry = dp * 32 + lax.broadcasted_iota(jnp.int32, (32, 128), 0)
        owner = source = length = jnp.zeros((32, 128), F32)
        for i in range(8):
            slots = S.i_route[i : i + 1, :]
            owner += jnp.where(at + i * 128 == entry, (slots // 32).astype(F32), 0.0)
            source += jnp.where(slots == entry, ((at + i * 128) // 32).astype(F32), 0.0)
            length += jnp.where(slots == entry, S.i_lengths[i : i + 1, :].astype(F32), 0.0)

        def column(table):
            return jnp.concatenate([jnp.sum(table, axis=1, keepdims=True)] * 4, axis=0)

        at = lax.broadcasted_iota(jnp.int32, (128, 128), 1)
        S.cols[...] = jnp.where(at == 0, column(owner), jnp.where(at == 1, column(source), column(length)))
        S.lanes[...] = S.cols[...].T
        own_rows = S.i_mem[...].astype(F32)
        S.a_out[...] = pack(0, jnp.concatenate([own_rows[:, j, :] for j in range(4)], axis=0).astype(BF))
        S.a_in[dp] = S.a_out[dp]
        waits.a = exchange(S.a_out, S.a_in, NDP, dp, lambda i: (i, tp), lambda i: i)

    def mask_cotangent():
        need(arriving.i_cot)

        @pl.loop(0, 4)
        def _(i):
            rows = pl.ds(pl.multiple_of(i * 16, 16), 16)
            live = lax.broadcasted_iota(jnp.int32, (16, D), 0) < jnp.full((16, D), target[i], jnp.int32)
            masked = jnp.where(live, S.i_cot[i].astype(F32), 0.0).astype(BF)
            for j in range(2):
                call[j, tp, rows] = masked[:, j * 2048 : j * 2048 + 2048]

    def place_examples():
        waits.a()
        mall[tp] = unpack(1, S.a_in[...].reshape(512, 128)).astype(BF)

    def queries():
        gather_n.done()
        need(arriving.wq)

        @pl.loop(0, 2)
        def _(i):
            rows = nall[pl.ds(i * 4, 4)].reshape(256, D)
            S.q[pl.ds(pl.multiple_of(i * 256, 256), 256), :] = jnp.dot(
                rows, S.wq[...], preferred_element_type=F32
            ).astype(BF)

    def keys_values():
        gather_m.done()
        need(arriving.wk, arriving.wv)
        for out, weight in ((S.k, S.wk), (S.v, S.wv)):
            total = jnp.zeros((128, HD), F32)
            for t in range(8):
                total += jnp.dot(mall[t], weight[t * 512 : t * 512 + 512, :], preferred_element_type=F32)
            out[...] = total.astype(BF)

    def attention():
        scores = lax.dot_general(S.q[...], S.k[...], NT_DIMS, preferred_element_type=F32) * (HD**-0.5)
        valid = (row // 16 == lane % 32) & (lane // 32 < S.lanes[2:3, :].astype(jnp.int32))
        scores = jnp.where(valid, scores, -1e30)
        expo = jnp.exp(scores - jnp.max(scores, axis=1, keepdims=True))
        expo = jnp.where(valid, expo, 0.0)
        S.p[...] = expo / jnp.sum(expo, axis=1, keepdims=True)
        context = jnp.dot(S.p[...].astype(BF), S.v[...], preferred_element_type=F32)
        S.ctx[...] = context.astype(BF).reshape(8, 64, HD)
        S.ctx_t[...] = context.T.astype(BF)

    def stacked(ref, core):
        return jnp.concatenate([ref[i * 2 + core] for i in range(NY)], axis=0)

    def wide_terms(ref, core, dst, product):
        @pl.loop(0, 8)
        def _(i):
            cols = pl.ds(pl.multiple_of(i * 512, 512), 512)
            dst[:, :, cols] = product(stacked(ref, core), cols).astype(BF).reshape(NY, 64, 512)

    def by_output(left, cols):
        need(arriving.wo)
        return jnp.dot(left, S.wo[:, cols], preferred_element_type=F32)

    def by_query(left, cols):
        return lax.dot_general(left, S.wq[cols, :], NT_DIMS, preferred_element_type=F32)

    def output_other():
        need(arriving.wo)
        wide_terms(S.ctx, other, S.sib_out, by_output)
        ring_a.send()

    def output_own():
        wide_terms(S.ctx, c, S.att, by_output)

    def output_ring():
        ring_a.start()
        pl.semaphore_signal(credit, 1, device_id=sib, device_id_type=MESH)

    def normed_other():
        ring_a.sent()
        wide_terms(S.gq, other, S.sib_out, by_query)
        pl.semaphore_wait(credit, 1)
        ring_g.send()

    def normed_own():
        wide_terms(S.gq, c, S.gn, by_query)

    def memory_terms(core, dst):
        @pl.loop(0, NY)
        def _(i):
            cols = pl.ds(pl.multiple_of((i * 2 + core) * 512, 512), 512)
            term = lax.dot_general(S.gk[...], S.wk[cols, :], NT_DIMS, preferred_element_type=F32)
            term += lax.dot_general(S.gv[...], S.wv[cols, :], NT_DIMS, preferred_element_type=F32)
            dst[i] = term.astype(BF)

    def memory_other():
        memory_terms(other, S.msib_out)
        ring_m.send()

    def memory_own():
        memory_terms(c, S.mt)

    def grad_context():
        gather_0.done()
        gather_1.done()
        need(arriving.wo)

        @pl.loop(0, 2)
        def _(i):
            total = None
            for j in range(2):
                rows = call[j, pl.ds(i * 4, 4)].reshape(256, 2048)
                cols = S.wo[:, j * 2048 : j * 2048 + 2048]
                term = lax.dot_general(rows, cols, NT_DIMS, preferred_element_type=F32)
                total = term if total is None else total + term
            S.gctx[pl.ds(pl.multiple_of(i * 256, 256), 256), :] = total.astype(BF)

    def grad_values():
        grad_v = jnp.dot(S.p[...].T.astype(BF), S.gctx[...], preferred_element_type=F32)
        S.gv[...] = grad_v.astype(BF)
        S.gv_t[...] = grad_v.T.astype(BF)

    def backward():
        probs = S.p[...]
        grad_p = lax.dot_general(S.gctx[...], S.v[...], NT_DIMS, preferred_element_type=F32)
        grad_s = probs * (grad_p - jnp.sum(probs * grad_p, axis=1, keepdims=True)) * (HD**-0.5)
        grad_q = jnp.dot(grad_s.astype(BF), S.k[...], preferred_element_type=F32)
        S.gq[...] = grad_q.astype(BF).reshape(8, 64, HD)
        S.gq_t[...] = grad_q.T.astype(BF)
        grad_k = jnp.dot(grad_s.T.astype(BF), S.q[...], preferred_element_type=F32)
        S.gk[...] = grad_k.astype(BF)
        S.gk_t[...] = grad_k.T.astype(BF)

    def context_first():
        gather_0.done()

        @pl.loop(0, 4)
        def _(i):
            to.tile(early * 2 + i // 2, lax.rem(i, 2))

        to.xf.start_far()

    def context_last():
        gather_1.done()

        @pl.loop(0, 4)
        def _(i):
            to.tile((1 - early) * 2 + i // 2, lax.rem(i, 2))

        to.xf.start_near()
        to.zf.start()

    def layer_result():
        ring_a.ring.arrive(2)

        @pl.loop(0, 4)
        def _(i):
            rows = pl.ds(pl.multiple_of(i * 16, 16), 16)
            S.r_layer[i] = (S.shifted[rows, :] + ring_a.ring.total(rows)).astype(BF)

        results.r_layer.start()

    def decoder_result():
        S.part[...] = jnp.zeros_like(S.part)
        ring_g.ring.arrive(2)

        @pl.loop(0, 4)
        def _(i):
            rows = pl.ds(pl.multiple_of(i * 16, 16), 16)
            grad = ring_g.ring.total(rows)
            inv = S.inv[rows, 0:1]
            normed = S.shifted[rows, :] * inv
            product = grad * normed
            wide_gain = S.gain[...]
            dot_mean = jnp.mean(wide_gain * product, axis=1, keepdims=True)
            masked = jnp.concatenate([call[j, tp, rows] for j in range(2)], axis=1)
            shift = masked.astype(F32) + inv * (wide_gain * grad - normed * dot_mean)
            S.r_dec[i] = shift.astype(BF)
            S.part[3] += product[0:8] + product[8:16]
            both = shift[0:8] + shift[8:16]
            kind = jnp.full((8, D), objective[i], jnp.int32)
            for j in range(3):
                S.part[j] += jnp.where(kind == j, both, 0.0)

        results.r_dec.start()
        for i in range(4):
            total = jnp.sum(S.part[i], axis=0, keepdims=True)
            for t in range(8):
                S.s_out[t, i : i + 1, :] = total[:, t * 512 : t * 512 + 256]
                S.s_out[t, i + 4 : i + 5, :] = total[:, t * 512 + 256 : t * 512 + 512]
        S.s_in[tp] = S.s_out[tp]
        waits.s = exchange(S.s_out, S.s_in, NT, tp, lambda i: (dp, i), lambda i: i)

    def sum_x():
        waits.s()
        S.s_x[x] = jnp.sum(S.s_in[...], axis=0)
        waits.x = exchange(S.s_x, S.s_x, NX, x, lambda i: (i * NZ + z, tp), lambda i: x)

    def sum_z():
        waits.x()
        S.s_z[z] = jnp.sum(S.s_x[...], axis=0)
        waits.z = exchange(S.s_z, S.s_z, NZ, z, lambda i: (x * NZ + i, tp), lambda i: z)

    def sum_t():
        waits.z()
        S.s_all[tp] = jnp.sum(S.s_z[...], axis=0)
        waits.t = exchange(S.s_all, S.s_all, NT, tp, lambda i: (dp, i), lambda i: tp)

    def small_results():
        waits.t()
        for t in range(8):
            S.r_mode[:, t * 512 : t * 512 + 256] = S.s_all[t, 0:3, :]
            S.r_mode[:, t * 512 + 256 : t * 512 + 512] = S.s_all[t, 4:7, :]
            for i in range(4):
                at, low = (i % 2) * 128, 3 + i // 2 * 4
                S.r_gain[t * 4 + i : t * 4 + i + 1, :] = S.s_all[t, low : low + 1, at : at + 128]
        results.r_mode.start()
        results.r_gain.start()

    def send_back():
        ring_m.ring.arrive(2)
        S.b_out[...] = pack(1, ring_m.ring.total(pl.ds(0, 128)).astype(BF))
        S.b_in[dp] = S.b_out[dp]
        waits.b = exchange(S.b_out, S.b_in, NDP, dp, lambda i: (i, tp), lambda i: i)

    def memory_result():
        waits.b()
        back = unpack(0, S.b_in[...].reshape(512, 128))
        for j in range(4):
            S.back[:, j, :] = back[j * 32 : j * 32 + 32]
        S.r_mem[...] = S.back[...].astype(BF)
        results.r_mem.start()

    gather_n.own()
    send_examples()
    place_examples()
    gather_m.own()
    gather_n.forward()
    mask_cotangent()
    gather_m.middle()
    gather_m.forward()
    gather_0.own()
    gather_0.forward()
    gather_n.middle()
    gather_m.far()
    gather_n.far()
    gather_1.own()
    gather_0.middle()
    queries()
    keys_values()
    attention()
    gather_0.far()
    output_other()
    gather_1.forward()
    context_first()
    output_own()
    gather_1.middle()
    gather_1.far()
    output_ring()
    context_last()
    grad_context()
    backward()
    tk.first()
    to.zf.step(1)
    tk.near()
    tk.own()
    to.xf.step(1)
    normed_other()
    grad_values()
    to.zf.step(2)
    tq.first()
    tq.near()
    tk.zf.step(1)
    tq.own()
    normed_own()
    to.zf.step(3)
    ring_g.start()
    tk.xf.step(1)
    tv.first()
    tv.near()
    tv.own()
    tq.zf.step(1)
    tk.zf.step(2)
    memory_other()
    to.to_z()
    tv.zf.step(1)
    tq.zf.step(2)
    ring_g.ring.step(1)
    tk.to_z()
    to.xs.step(1)
    tv.zf.step(2)
    tq.xf.step(1)
    ring_a.ring.step(1)
    tk.xs.step(1)
    tk.zf.step(3)
    tq.zf.step(3)
    tv.xf.step(1)
    tk.xs.step(2)
    decoder_result()
    tv.zf.step(3)
    memory_own()
    tq.to_z()
    to.to_x()
    tk.to_x()
    ring_m.start()
    to.xs.step(2)
    tk.xs.step(3)
    sum_x()
    tv.to_z()
    tq.to_x()
    layer_result()
    ring_m.ring.step(1)
    tq.xs.step(1)
    tv.to_x()
    to.xs.step(3)
    tk.zs.step(1)
    tv.xs.step(1)
    tq.zs.step(1)
    sum_z()
    tq.xs.step(2)
    tv.xs.step(2)
    send_back()
    to.zs.step(1)
    tv.zs.step(1)
    tk.result(results.r_k)
    sum_t()
    tv.xs.step(3)
    tq.xs.step(3)
    small_results()
    to.result(results.r_o)
    memory_result()
    tv.result(results.r_v)
    tq.result(results.r_q)

    links.finish_sends()
    for one in vars(results).values():
        one.wait()


def place(*refs):
    count = len(RESULTS)
    held, sems = refs[2 * count : 3 * count], refs[3 * count]
    into = [pltpu.make_async_copy(refs[i], held[i], sems.at[0, i]) for i in range(count)]
    out = [pltpu.make_async_copy(held[i], refs[count + i], sems.at[1, i]) for i in range(count)]
    for one in into:
        one.start()
    for one, then in zip(into, out):
        one.wait()
        then.start()
    for one in out:
        one.wait()


def shards(
    decoder_states,
    encoder_memory,
    memory_route,
    memory_length,
    target_length,
    objective,
    mode_table,
    norm_gain,
    w_query,
    w_key,
    w_value,
    w_output,
    cotangent,
):
    smem = pl.BlockSpec(memory_space=pltpu.SMEM)
    hbm = pl.BlockSpec(memory_space=pl.ANY)
    out_shape = [jax.ShapeDtypeStruct(*one) for one in RESULTS.values()]
    found = pl.pallas_call(
        kernel,
        out_shape=out_shape,
        in_specs=[smem] * 2 + [hbm] * len(SOURCES),
        out_specs=[hbm] * len(RESULTS),
        scratch_shapes=[pltpu.VMEM(*one) for one in FLAT]
        + [
            pltpu.SemaphoreType.DMA((NSEND,)),
            pltpu.SemaphoreType.DMA((NRECV,)),
            pltpu.SemaphoreType.DMA((len(SOURCES) + len(RESULTS),)),
            pltpu.SemaphoreType.REGULAR,
        ],
        compiler_params=pltpu.CompilerParams(
            collective_id=0, has_side_effects=True, vmem_limit_bytes=62 * 1024 * 1024
        ),
        cost_estimate=pl.CostEstimate(flops=8 * 10**9, bytes_accessed=12 * 10**6, transcendentals=10**5),
    )(
        target_length,
        objective,
        mode_table,
        norm_gain.reshape(32, 128),
        decoder_states,
        memory_route.reshape(8, 128),
        memory_length.reshape(8, 128),
        encoder_memory,
        cotangent,
        w_query,
        w_key,
        w_value,
        w_output,
    )
    layer, dec, mem, gq, gk, gv, go, gain, mode = pl.pallas_call(
        place,
        out_shape=out_shape,
        in_specs=[hbm] * len(RESULTS),
        out_specs=[hbm] * len(RESULTS),
        scratch_shapes=[pltpu.VMEM(*one) for one in RESULTS.values()]
        + [pltpu.SemaphoreType.DMA((2, len(RESULTS)))],
    )(*found)
    return layer, dec, mem, gq, gk, gv, go, gain.reshape(D), mode


def solution(mesh):
    return jax.shard_map(
        shards,
        mesh=mesh,
        in_specs=(
            P(("dp", "tensor"), None, None),
            P("dp", None, "tensor"),
            P(),
            P(),
            P(("dp", "tensor")),
            P(("dp", "tensor")),
            P(),
            P(),
            P(None, "tensor"),
            P(None, "tensor"),
            P(None, "tensor"),
            P("tensor", None),
            P(("dp", "tensor"), None, None),
        ),
        out_specs=(
            P(("dp", "tensor"), None, None),
            P(("dp", "tensor"), None, None),
            P("dp", None, "tensor"),
            P("dp", "tensor"),
            P("dp", "tensor"),
            P("dp", "tensor"),
            P("tensor", "dp"),
            P(),
            P(),
        ),
        check_vma=False,
    )
```
